32 devices in a mesh: groups: 2 (over x), expert: 8 (over z, y), tensor: 2 (over core).
Axes of the slice: x: 2, y: 2, z: 4, core: 2. Of those that a mesh axis runs over, the one named last changes fastest.
Arguments:
- tokens: bfloat16 [4, 512, 2048], P(None, ('groups', 'expert')), parts along dimension 1, may hold values from -6 to 6
- routes: int32 [4, 512, 8], P(None, ('groups', 'expert')), parts along dimension 1, may hold values from 0 to 31, all different within a row; in each aligned block of 32 rows (0 to 31, 32 to 63, ..., all dimensions but the last counted through in order) at most 16 rows name the same one
- mixing: float32 [4, 512, 8], P(None, ('groups', 'expert')), parts along dimension 1, may hold values from 0.1 to 0.4
- gate_weight: bfloat16 [32, 4096, 768], P(None, ('groups', 'expert', 'tensor')), parts along dimension 1, may hold values from -0.125 to 0.125
- up_weight: bfloat16 [32, 4096, 768], P(None, ('groups', 'expert', 'tensor')), parts along dimension 1, may hold values from -0.125 to 0.125
- down_weight: bfloat16 [32, 4096, 768], P(None, ('groups', 'expert', 'tensor')), parts along dimension 1, may hold values from -0.21875 to 0.21875
Outputs:
- block_out: bfloat16 [4, 512, 2048], P(None, ('groups', 'expert'), 'tensor'), parts along dimension 1
The draws below stay inside these ranges and needn't reach their ends.
There are 2 independent parts, one for each index of `groups`. The reference program is written for one: setup_inputs(seed, part) draws one part's arguments, and reference() takes and returns one part's arrays. A program takes and returns all parts, laid end to end along the dimension named above; each array names one. Nothing has to cross between parts.
Inputs may be any that keep to these rules, and one draw needn't show every extreme that they name: `routes`: in every step each row names 8 different experts, and within each aligned block of 32 rows (the rows of one index of expert) no expert is named by more than 16 rows, a bound that some block reaches.
All inputs are finite; a program needn't handle non-finite values.
Results may differ from the reference program's by a relative error of at most 0.0058.
Values may be sent and summed in bfloat16 or wider, within the bound.
A program may use at most 192 MiB of HBM per device.

```python
import math
import jax
import jax.numpy as jnp
import numpy as np
from jax import lax

D = 2048
FF = 768
TOPK = 8
STEPS = 4
ROWS_DEV = 32
EXPERTS = 32
CAP = 16
TOKENS = 256
N_EXPERT = 8


def shard_levels(stream_key, dims, pieces, smallest, top_value):
    factor_of, own = 1.0, jax.random.fold_in(stream_key, 6)
    for dim, parts in pieces:
        steps = jnp.exp(jax.random.uniform(jax.random.fold_in(own, dim), (parts,), jnp.float32, smallest / len(pieces), top_value / len(pieces)))
        factor_of = factor_of * jnp.repeat(steps, dims[dim] // parts).reshape([-1 if axis == dim else 1 for axis in range(len(dims))])
    return factor_of


def shared_out(own_key, own, number, rows, number_of, top, limit, lean):
    order = jax.random.permutation(own_key, number_of)
    heavy_load, usual = portions_of(number_of, rows * top, limit, lean, True), portions_of(number_of, rows * top, limit, lean, False)
    places = jnp.arange(number_of)

    def named(sizes, turn):
        used = int((sizes > 0).sum())
        fixed = max(1, used // 4)
        moved = fixed + (places - fixed + turn * (used - fixed)) % max(1, number_of - fixed)
        return jnp.zeros((number_of,), jnp.int32).at[order[jnp.where(places < fixed, places, moved)]].set(jnp.asarray(sizes, jnp.int32))

    sizes = jnp.where(number % 4 == 0, named(heavy_load, number // 4), named(usual, number - number // 4 - 1))
    mixed = jax.random.permutation(jax.random.fold_in(own, 3), number_of)
    giver, receiver = mixed[0:number_of // 2 * 2:2], mixed[1:number_of // 2 * 2:2]
    margin = jnp.minimum(sizes[giver] - 1, limit - sizes[receiver]) // 2
    margin = jnp.where((giver == order[0]) | (receiver == order[0]) | (sizes[receiver] == 0), 0, jnp.maximum(margin, 0))
    moved = jax.random.randint(jax.random.fold_in(own, 4), (number_of // 2,), 0, 1 << 20) % (margin + 1)
    sizes = sizes.at[giver].add(-moved).at[receiver].add(moved)
    labels = jnp.searchsorted(jnp.cumsum(sizes), jnp.arange(rows * top), side="right").astype(jnp.int32)
    grid = labels.reshape(top, rows).T
    grid = grid[jax.random.permutation(jax.random.fold_in(own, 1), rows)]
    turn = jax.random.randint(jax.random.fold_in(own, 2), (rows, 1), 0, top)
    return jnp.take_along_axis(grid, (jnp.arange(top)[None, :] + turn) % top, axis=1)


def portions_of(amount, total, reach, lean, full):
    loads = [(1 << 20) // math.isqrt(rank ** lean) + 1 for rank in range(1, amount + 1)]
    largest = reach if full else min(reach, max(-(-total // amount), total * loads[0] // sum(loads)))
    least = 1 if total - largest >= amount - 1 else 0
    holding, surplus = [largest] + [least] * (amount - 1), total - largest - least * (amount - 1)
    while surplus > 0:
        movable = [i for i in range(1, amount) if holding[i] < largest] or [i for i in range(1, amount) if holding[i] < reach]
        mass, left = sum([loads[i] for i in movable]), surplus
        for i in movable:
            more = min(reach - holding[i], max(1, left * loads[i] // mass), surplus)
            holding[i] = holding[i] + more
            surplus = surplus - more
    return np.array(holding)


def normal_values(key, shape, deviation, bound, pieces=(), kind=jnp.bfloat16):
    drawn = jax.random.normal(key, shape, jnp.float32) * deviation
    if len(pieces) > 0:
        drawn = shard_levels(key, shape, pieces, -0.22, 0.18) * drawn
    return jnp.clip(drawn, min=-bound, max=bound).astype(kind)


def setup_inputs(seed: int = 0, part: int = 0) -> dict:
    key_list = jax.random.split(jax.random.key(seed), 7)
    part_keys = jax.random.split(jax.random.fold_in(key_list[6], part), 7)
    tokens = normal_values(part_keys[0], (STEPS, TOKENS, D), 1.0, 6.0, ((1, 8),))
    routes_keys = jax.random.split(jax.random.fold_in(part_keys[1], 1), STEPS * TOKENS // ROWS_DEV)
    routes_turns = jax.random.permutation(jax.random.fold_in(part_keys[1], 3), STEPS * TOKENS // ROWS_DEV)
    routes = jax.vmap(lambda own, number: shared_out(jax.random.fold_in(part_keys[1], 2), own, number, ROWS_DEV, EXPERTS, TOPK, CAP, 2))(routes_keys, routes_turns).reshape((STEPS, TOKENS, TOPK))
    mixing = jnp.clip(0.1 + 0.3 * jax.random.uniform(part_keys[2], (STEPS, TOKENS, TOPK), jnp.float32) ** shard_levels(part_keys[2], (STEPS, TOKENS, TOPK), ((1, 8),), -0.2, 0.2), 0.1, 0.4)
    gate_weight = normal_values(part_keys[3], (EXPERTS, D, FF), D ** -0.5, 0.125, ((1, 16),))
    up_weight = normal_values(part_keys[4], (EXPERTS, D, FF), D ** -0.5, 0.125, ((1, 16),))
    down_weight = normal_values(part_keys[5], (EXPERTS, D, FF), FF ** -0.5, 0.21875, ((1, 16),))
    return dict(tokens=tokens, routes=routes, mixing=mixing, gate_weight=gate_weight, up_weight=up_weight, down_weight=down_weight)


def ranks_of(chosen, expert_count):
    onehot_table = (chosen[:, None] == jnp.arange(expert_count, dtype=jnp.int32)[None, :]).astype(jnp.int32)
    before = jnp.cumsum(onehot_table, axis=0) - onehot_table
    return jnp.sum(before * onehot_table, axis=1).astype(jnp.int32)


def expert_apply(operands):
    rows_in, gate_w, up_w, down_w = operands
    gate_act = jnp.dot(rows_in, gate_w, preferred_element_type=jnp.float32)
    up_act = jnp.dot(rows_in, up_w, preferred_element_type=jnp.float32)
    hidden_act = (jax.nn.silu(gate_act) * up_act).astype(jnp.bfloat16)
    return lax.dot_general(hidden_act, down_w, (((1,), (1,)), ((), ())), preferred_element_type=jnp.float32).astype(jnp.bfloat16)


def reference(tokens, routes, mixing, gate_weight, up_weight, down_weight):
    results = []
    for step_id in range(STEPS):
        inputs = tokens[step_id]
        blocks = routes[step_id].reshape(N_EXPERT, ROWS_DEV * TOPK)
        rank_index = jax.vmap(lambda chosen: ranks_of(chosen, EXPERTS))(blocks)
        anchor = jnp.arange(N_EXPERT, dtype=jnp.int32)[:, None]
        slot_index = (blocks * (N_EXPERT * CAP) + anchor * CAP + rank_index).reshape(-1).astype(jnp.int32)
        repeated = jnp.repeat(inputs, TOPK, axis=0)
        buffer = jnp.zeros((EXPERTS * N_EXPERT * CAP, D), jnp.bfloat16).at[slot_index].set(repeated)
        buffer = buffer.reshape(EXPERTS, N_EXPERT * CAP, D)
        outputs = lax.map(expert_apply, (buffer, gate_weight, up_weight, down_weight))
        picked = outputs.reshape(EXPERTS * N_EXPERT * CAP, D)[slot_index].reshape(TOKENS, TOPK, D).astype(jnp.float32)
        combined = jnp.sum(mixing[step_id][:, :, None] * picked, axis=1)
        results.append(combined.astype(jnp.bfloat16))
    return jnp.stack(results)
```

```python
import jax
import jax.numpy as jnp
from jax import lax
from jax.sharding import PartitionSpec as P

ALL = ("expert", "tensor")


def own_experts(weight):
    devices = lax.axis_size("expert") * lax.axis_size("tensor")
    expert_count, rows_block, hidden_all = weight.shape
    local_count = expert_count // devices
    parts = weight.reshape(devices, local_count, rows_block, hidden_all)
    moved = lax.all_to_all(parts, ALL, split_axis=0, concat_axis=0, tiled=True)
    return moved.transpose(1, 0, 2, 3).reshape(local_count, devices * rows_block, hidden_all)


def local(tokens, routes, mixing, gate_weight, up_weight, down_weight):
    owners = lax.axis_size("expert")
    pairs = lax.axis_size("tensor")
    expert_count = gate_weight.shape[0]
    step_count, row_count, model_width = tokens.shape
    local_count = expert_count // (owners * pairs)
    block = step_count * row_count
    named = routes[..., None] == jnp.arange(expert_count, dtype=jnp.int32)
    shares = jnp.sum(jnp.where(named, mixing[..., None], 0.0), axis=2)
    rows_all = lax.all_gather(tokens.reshape(block, model_width), "expert", axis=0, tiled=True)
    shares_all = lax.all_gather(shares.reshape(block, expert_count), "expert", axis=0, tiled=True)
    me = lax.axis_index("expert") * pairs + lax.axis_index("tensor")
    own_shares = lax.dynamic_slice_in_dim(shares_all, me * local_count, local_count, axis=1)
    w_gate = own_experts(gate_weight)
    w_up = own_experts(up_weight)
    w_down = own_experts(down_weight)
    total = jnp.zeros((owners * block, model_width), jnp.float32)
    for k in range(local_count):
        gate_act = jnp.dot(rows_all, w_gate[k], preferred_element_type=jnp.float32)
        up_act = jnp.dot(rows_all, w_up[k], preferred_element_type=jnp.float32)
        hidden_act = (jax.nn.silu(gate_act) * up_act * own_shares[:, k : k + 1]).astype(jnp.bfloat16)
        total = total + lax.dot_general(
            hidden_act, w_down[k], (((1,), (1,)), ((), ())), preferred_element_type=jnp.float32
        )
    half = model_width // pairs
    sent = total.reshape(owners * block, pairs, half).transpose(1, 0, 2).astype(jnp.bfloat16)
    both = lax.all_to_all(sent, "tensor", split_axis=0, concat_axis=0, tiled=True)
    chip_sum = jnp.sum(both.astype(jnp.float32), axis=0).astype(jnp.bfloat16)
    returned = lax.all_to_all(
        chip_sum.reshape(owners, block, half), "expert", split_axis=0, concat_axis=0, tiled=True
    )
    out = jnp.sum(returned.astype(jnp.float32), axis=0).astype(jnp.bfloat16)
    return out.reshape(step_count, row_count, half)


def solution(mesh):
    return jax.shard_map(
        local,
        mesh=mesh,
        in_specs=(
            P(None, ("groups", "expert"), None),
            P(None, ("groups", "expert"), None),
            P(None, ("groups", "expert"), None),
            P(None, ("groups", "expert", "tensor"), None),
            P(None, ("groups", "expert", "tensor"), None),
            P(None, ("groups", "expert", "tensor"), None),
        ),
        out_specs=P(None, ("groups", "expert"), "tensor"),
        check_vma=False,
    )
```

```python
import jax
import jax.numpy as jnp
from jax import lax
from jax.sharding import PartitionSpec as P

ALL = ("expert", "tensor")


def own_experts(weight):
    devices = lax.axis_size("expert") * lax.axis_size("tensor")
    expert_count, rows_block, hidden_all = weight.shape
    local_count = expert_count // devices
    parts = weight.reshape(devices, local_count, rows_block, hidden_all)
    moved = lax.all_to_all(parts, ALL, split_axis=0, concat_axis=0, tiled=True)
    return moved.transpose(1, 0, 2, 3).reshape(local_count, devices * rows_block, hidden_all)


def swap(value, axis, distance):
    count = lax.axis_size(axis)
    return lax.ppermute(value, axis, [(i, i ^ distance) for i in range(count)])


def distances_of(owners):
    found, distance = [], owners // 2
    while distance >= 1:
        found.append(distance)
        distance //= 2
    return found


def local(tokens, routes, mixing, gate_weight, up_weight, down_weight):
    owners = lax.axis_size("expert")
    pairs = lax.axis_size("tensor")
    expert_count = gate_weight.shape[0]
    step_count, row_count, model_width = tokens.shape
    devices = owners * pairs
    local_count = expert_count // devices
    block = step_count * row_count
    half = model_width // pairs
    side = lax.axis_index("tensor")
    me = lax.axis_index("expert") * pairs + side
    named = routes[..., None] == jnp.arange(expert_count, dtype=jnp.int32)
    shares = jnp.sum(jnp.where(named, mixing[..., None], 0.0), axis=2).reshape(block, expert_count)
    x_half = lax.dynamic_slice_in_dim(tokens.reshape(block, model_width), side * half, half, axis=1)
    for distance in distances_of(owners):
        x_half = jnp.concatenate([x_half, swap(x_half, "expert", distance)], axis=0)
        shares = jnp.concatenate([shares, swap(shares, "expert", distance)], axis=0)
    x_other = swap(x_half, "tensor", 1)
    rows_all = jnp.concatenate(
        [jnp.where(side == 0, x_half, x_other), jnp.where(side == 0, x_other, x_half)], axis=1
    )
    own_shares = lax.dynamic_slice_in_dim(shares, me * local_count, local_count, axis=1)

    w_gate = own_experts(gate_weight)
    up_weight, rows_all, w_gate = lax.optimization_barrier((up_weight, rows_all, w_gate))
    w_up = own_experts(up_weight)
    down_weight, w_up = lax.optimization_barrier((down_weight, w_up))
    down_parts = down_weight.reshape(devices, local_count, *down_weight.shape[1:])
    hidden = []
    for k in range(local_count):
        gate_act = jnp.dot(rows_all, w_gate[k], preferred_element_type=jnp.float32)
        up_act = jnp.dot(rows_all, w_up[k], preferred_element_type=jnp.float32)
        hidden.append(
            (jax.nn.silu(gate_act) * up_act * own_shares[:, k : k + 1]).astype(jnp.bfloat16)
        )
    total = None
    for k in range(local_count):
        piece = down_parts[:, k]
        if k > 0:
            piece, w_down = lax.optimization_barrier((piece, w_down))
        moved = lax.all_to_all(piece, ALL, split_axis=0, concat_axis=0, tiled=True)
        w_down = moved.reshape(model_width, moved.shape[2])
        part = lax.dot_general(
            hidden[k], w_down, (((1,), (1,)), ((), ())), preferred_element_type=jnp.float32
        )
        total = part if total is None else total + part
    kept = lax.dynamic_slice_in_dim(total, side * half, half, axis=1)
    given = lax.dynamic_slice_in_dim(total, (1 - side) * half, half, axis=1).astype(jnp.bfloat16)
    kept = kept + swap(given, "tensor", 1).astype(jnp.float32)
    for distance in reversed(distances_of(owners)):
        count = kept.shape[0] // 2
        got = swap(kept[count:].astype(jnp.bfloat16), "expert", distance)
        kept = kept[:count] + got.astype(jnp.float32)
    return kept.astype(jnp.bfloat16).reshape(step_count, row_count, half)


def solution(mesh):
    return jax.shard_map(
        local,
        mesh=mesh,
        in_specs=(
            P(None, ("groups", "expert"), None),
            P(None, ("groups", "expert"), None),
            P(None, ("groups", "expert"), None),
            P(None, ("groups", "expert", "tensor"), None),
            P(None, ("groups", "expert", "tensor"), None),
            P(None, ("groups", "expert", "tensor"), None),
        ),
        out_specs=P(None, ("groups", "expert"), "tensor"),
        check_vma=False,
    )
```

```python
import jax
import jax.numpy as jnp
from jax import lax
from jax.sharding import PartitionSpec as P

ALL = ("expert", "tensor")


def own_experts(weight):
    devices = lax.axis_size("expert") * lax.axis_size("tensor")
    expert_count, rows_block, hidden_all = weight.shape
    local_count = expert_count // devices
    parts = weight.reshape(devices, local_count, rows_block, hidden_all)
    moved = lax.all_to_all(parts, ALL, split_axis=0, concat_axis=0, tiled=True)
    return moved.transpose(1, 0, 2, 3).reshape(local_count, devices * rows_block, hidden_all)


def swap(value, axis, distance):
    count = lax.axis_size(axis)
    return lax.ppermute(value, axis, [(i, i ^ distance) for i in range(count)])


def orders_of(owners):
    bits = [bit for bit in range(owners.bit_length() - 1)][::-1]
    return bits, bits[:1] + bits[1:][::-1]


def doubled(value, order):
    count = len(order)
    value = value.reshape((1,) * count + value.shape)
    for bit in order:
        value = jnp.concatenate([value, swap(value, "expert", 1 << bit)], axis=bit)
    return value.reshape(-1, value.shape[-1])


def halved(value, order, block):
    value = value.reshape((2,) * len(order) + (block, value.shape[-1]))
    for bit in order[::-1]:
        near = lax.slice_in_dim(value, 0, 1, axis=bit)
        far = lax.slice_in_dim(value, 1, 2, axis=bit).astype(jnp.bfloat16)
        value = near + swap(far, "expert", 1 << bit).astype(jnp.float32)
    return value.reshape(block, value.shape[-1])


def local(tokens, routes, mixing, gate_weight, up_weight, down_weight):
    owners = lax.axis_size("expert")
    pairs = lax.axis_size("tensor")
    expert_count = gate_weight.shape[0]
    step_count, row_count, model_width = tokens.shape
    devices = owners * pairs
    local_count = expert_count // devices
    block = step_count * row_count
    half = model_width // pairs
    quarter = half // 2
    side = lax.axis_index("tensor")
    me = lax.axis_index("expert") * pairs + side
    orders = orders_of(owners)
    named = routes[..., None] == jnp.arange(expert_count, dtype=jnp.int32)
    shares = jnp.sum(jnp.where(named, mixing[..., None], 0.0), axis=2).reshape(block, expert_count)
    x_half = lax.dynamic_slice_in_dim(tokens.reshape(block, model_width), side * half, half, axis=1)
    x_half = jnp.concatenate(
        [doubled(x_half[:, :quarter], orders[0]), doubled(x_half[:, quarter:], orders[1])], axis=1
    )
    shares = doubled(shares, orders[0])
    x_half, shares, gate_weight = lax.optimization_barrier((x_half, shares, gate_weight))
    x_other = swap(x_half, "tensor", 1)
    rows_all = jnp.concatenate(
        [jnp.where(side == 0, x_half, x_other), jnp.where(side == 0, x_other, x_half)], axis=1
    )
    own_shares = lax.dynamic_slice_in_dim(shares, me * local_count, local_count, axis=1)

    w_gate = own_experts(gate_weight)
    up_weight, w_gate = lax.optimization_barrier((up_weight, w_gate))
    w_up = own_experts(up_weight)
    down_weight, w_up = lax.optimization_barrier((down_weight, w_up))
    down_parts = down_weight.reshape(devices, local_count, *down_weight.shape[1:])
    hidden = []
    for k in range(local_count):
        gate_act = jnp.dot(rows_all, w_gate[k], preferred_element_type=jnp.float32)
        up_act = jnp.dot(rows_all, w_up[k], preferred_element_type=jnp.float32)
        hidden.append(
            (jax.nn.silu(gate_act) * up_act * own_shares[:, k : k + 1]).astype(jnp.bfloat16)
        )
    sums = [None, None]
    for k in range(local_count):
        piece = down_parts[:, k]
        if k > 0:
            piece, w_down = lax.optimization_barrier((piece, w_down))
        moved = lax.all_to_all(piece, ALL, split_axis=0, concat_axis=0, tiled=True)
        w_down = moved.reshape(model_width, moved.shape[2])
        for index, part_side in enumerate((1 - side, side)):
            w_part = lax.dynamic_slice_in_dim(w_down, part_side * half, half, axis=0)
            part = lax.dot_general(
                hidden[k], w_part, (((1,), (1,)), ((), ())), preferred_element_type=jnp.float32
            )
            sums[index] = part if sums[index] is None else sums[index] + part
    given, kept = sums
    kept = kept + swap(given.astype(jnp.bfloat16), "tensor", 1).astype(jnp.float32)
    out = jnp.concatenate(
        [
            halved(kept[:, :quarter], orders[0], block),
            halved(kept[:, quarter:], orders[1], block),
        ],
        axis=1,
    )
    return out.astype(jnp.bfloat16).reshape(step_count, row_count, half)


def solution(mesh):
    return jax.shard_map(
        local,
        mesh=mesh,
        in_specs=(
            P(None, ("groups", "expert"), None),
            P(None, ("groups", "expert"), None),
            P(None, ("groups", "expert"), None),
            P(None, ("groups", "expert", "tensor"), None),
            P(None, ("groups", "expert", "tensor"), None),
            P(None, ("groups", "expert", "tensor"), None),
        ),
        out_specs=P(None, ("groups", "expert"), "tensor"),
        check_vma=False,
    )
```

```python
import jax
import jax.numpy as jnp
from jax import lax
from jax.sharding import PartitionSpec as P

ALL = ("expert", "tensor")


def swap(value, axis, distance):
    count = lax.axis_size(axis)
    return lax.ppermute(value, axis, [(i, i ^ distance) for i in range(count)])


def orders_of(owners):
    bits = [bit for bit in range(owners.bit_length() - 1)][::-1]
    return bits, bits[:1] + bits[1:][::-1]


def doubled(value, bit):
    return jnp.concatenate([value, swap(value, "expert", 1 << bit)], axis=bit)


def halved(value, order, block):
    value = value.reshape((2,) * len(order) + (block, value.shape[-1]))
    for bit in order[::-1]:
        near = lax.slice_in_dim(value, 0, 1, axis=bit)
        far = lax.slice_in_dim(value, 1, 2, axis=bit).astype(jnp.bfloat16)
        value = near + swap(far, "expert", 1 << bit).astype(jnp.float32)
    return value.reshape(block, value.shape[-1])


def local(tokens, routes, mixing, gate_weight, up_weight, down_weight):
    owners = lax.axis_size("expert")
    pairs = lax.axis_size("tensor")
    expert_count = gate_weight.shape[0]
    step_count, row_count, model_width = tokens.shape
    devices = owners * pairs
    local_count = expert_count // devices
    block = step_count * row_count
    half = model_width // pairs
    quarter = half // 2
    side = lax.axis_index("tensor")
    me = lax.axis_index("expert") * pairs + side
    orders = orders_of(owners)
    named = routes[..., None] == jnp.arange(expert_count, dtype=jnp.int32)
    shares = jnp.sum(jnp.where(named, mixing[..., None], 0.0), axis=2).reshape(block, expert_count)
    x_half = lax.dynamic_slice_in_dim(tokens.reshape(block, model_width), side * half, half, axis=1)
    ones = (1,) * len(orders[0])
    state = (
        x_half[:, :quarter].reshape(ones + (block, quarter)),
        x_half[:, quarter:].reshape(ones + (block, half - quarter)),
        shares.reshape(ones + (block, expert_count)),
    )

    def advance(state, stage):
        if stage < len(orders[0]):
            first, second = orders[0][stage], orders[1][stage]
            return doubled(state[0], first), doubled(state[1], second), doubled(state[2], first)
        x_half = jnp.concatenate(
            [state[0].reshape(-1, quarter), state[1].reshape(-1, half - quarter)], axis=1
        )
        return x_half, swap(x_half, "tensor", 1), state[2].reshape(-1, expert_count)

    stages = len(orders[0]) + 1
    pieces = []
    for weight in (gate_weight, up_weight, down_weight):
        parts = weight.reshape(devices, local_count, *weight.shape[1:])
        pieces += [parts[:, k] for k in range(local_count)]
    moved = []
    for index, piece in enumerate(pieces):
        if index > 0 and index <= stages:
            piece, state, moved[-1] = lax.optimization_barrier((piece, state, moved[-1]))
        elif index > 0:
            piece, moved[-1] = lax.optimization_barrier((piece, moved[-1]))
        if index < stages:
            state = advance(state, index)
        moved.append(lax.all_to_all(piece, ALL, split_axis=0, concat_axis=0, tiled=True))
    for stage in range(len(pieces), stages):
        state = advance(state, stage)
    x_half, x_other, shares = state
    rows_all = jnp.concatenate(
        [jnp.where(side == 0, x_half, x_other), jnp.where(side == 0, x_other, x_half)], axis=1
    )
    own_shares = lax.dynamic_slice_in_dim(shares, me * local_count, local_count, axis=1)
    moved = [value.reshape(model_width, value.shape[2]) for value in moved]
    w_gate, w_up, w_downs = [
        moved[i * local_count : (i + 1) * local_count] for i in range(3)
    ]
    hidden = []
    for k in range(local_count):
        gate_act = jnp.dot(rows_all, w_gate[k], preferred_element_type=jnp.float32)
        up_act = jnp.dot(rows_all, w_up[k], preferred_element_type=jnp.float32)
        hidden.append(
            (jax.nn.silu(gate_act) * up_act * own_shares[:, k : k + 1]).astype(jnp.bfloat16)
        )
    sums = [None, None]
    for k in range(local_count):
        w_down = w_downs[k]
        for index, part_side in enumerate((1 - side, side)):
            w_part = lax.dynamic_slice_in_dim(w_down, part_side * half, half, axis=0)
            part = lax.dot_general(
                hidden[k], w_part, (((1,), (1,)), ((), ())), preferred_element_type=jnp.float32
            )
            sums[index] = part if sums[index] is None else sums[index] + part
    given, kept = sums
    kept = kept + swap(given.astype(jnp.bfloat16), "tensor", 1).astype(jnp.float32)
    out = jnp.concatenate(
        [
            halved(kept[:, :quarter], orders[0], block),
            halved(kept[:, quarter:], orders[1], block),
        ],
        axis=1,
    )
    return out.astype(jnp.bfloat16).reshape(step_count, row_count, half)


def solution(mesh):
    return jax.shard_map(
        local,
        mesh=mesh,
        in_specs=(
            P(None, ("groups", "expert"), None),
            P(None, ("groups", "expert"), None),
            P(None, ("groups", "expert"), None),
            P(None, ("groups", "expert", "tensor"), None),
            P(None, ("groups", "expert", "tensor"), None),
            P(None, ("groups", "expert", "tensor"), None),
        ),
        out_specs=P(None, ("groups", "expert"), "tensor"),
        check_vma=False,
    )
```

```python
import jax
import jax.numpy as jnp
from jax import lax
from jax.sharding import PartitionSpec as P

ALL = ("expert", "tensor")


def swap(value, axis, distance):
    count = lax.axis_size(axis)
    return lax.ppermute(value, axis, [(i, i ^ distance) for i in range(count)])


def orders_of(owners):
    bits = [bit for bit in range(owners.bit_length() - 1)][::-1]
    return bits, bits[:1] + bits[1:][::-1]


def doubled(value, bit):
    return jnp.concatenate([value, swap(value, "expert", 1 << bit)], axis=bit)


def halved(value, order, block):
    value = value.reshape((2,) * len(order) + (block, value.shape[-1]))
    for bit in order[::-1]:
        near = lax.slice_in_dim(value, 0, 1, axis=bit)
        far = lax.slice_in_dim(value, 1, 2, axis=bit).astype(jnp.bfloat16)
        value = near + swap(far, "expert", 1 << bit).astype(jnp.float32)
    return value.reshape(block, value.shape[-1])


def local(tokens, routes, mixing, gate_weight, up_weight, down_weight):
    owners = lax.axis_size("expert")
    pairs = lax.axis_size("tensor")
    expert_count = gate_weight.shape[0]
    step_count, row_count, model_width = tokens.shape
    devices = owners * pairs
    local_count = expert_count // devices
    block = step_count * row_count
    half = model_width // pairs
    quarter = half // 2
    side = lax.axis_index("tensor")
    me = lax.axis_index("expert") * pairs + side
    orders = orders_of(owners)
    named = routes[..., None] == jnp.arange(expert_count, dtype=jnp.int32)
    shares = jnp.sum(jnp.where(named, mixing[..., None], 0.0), axis=2).reshape(block, expert_count)
    x_half = lax.dynamic_slice_in_dim(tokens.reshape(block, model_width), side * half, half, axis=1)
    ones = (1,) * len(orders[0])
    state = (
        x_half[:, :quarter].reshape(ones + (block, quarter)),
        x_half[:, quarter:].reshape(ones + (block, half - quarter)),
        shares.reshape(ones + (block, expert_count)),
    )

    def advance(state, stage):
        if stage < len(orders[0]):
            first, second = orders[0][stage], orders[1][stage]
            return doubled(state[0], first), doubled(state[1], second), doubled(state[2], first)
        x_half = jnp.concatenate(
            [state[0].reshape(-1, quarter), state[1].reshape(-1, half - quarter)], axis=1
        )
        return x_half, swap(x_half, "tensor", 1), state[2].reshape(-1, expert_count)

    stages = len(orders[0]) + 1
    pieces = []
    for weight in (gate_weight, up_weight, down_weight):
        pieces += [weight[k * devices : (k + 1) * devices] for k in range(local_count)]
    moved = []
    for index, piece in enumerate(pieces):
        if index > 1 and index <= stages:
            piece, state, moved[-2] = lax.optimization_barrier((piece, state, moved[-2]))
        elif index > 1:
            piece, moved[-2] = lax.optimization_barrier((piece, moved[-2]))
        if index < stages:
            state = advance(state, index)
        moved.append(lax.all_to_all(piece, ALL, split_axis=0, concat_axis=0, tiled=True))
    for stage in range(len(pieces), stages):
        state = advance(state, stage)
    x_half, x_other, shares = state
    rows_all = jnp.concatenate(
        [jnp.where(side == 0, x_half, x_other), jnp.where(side == 0, x_other, x_half)], axis=1
    )
    own_shares = [
        lax.dynamic_slice_in_dim(shares, k * devices + me, 1, axis=1) for k in range(local_count)
    ]
    moved = [value.reshape(model_width, value.shape[2]) for value in moved]
    w_gate, w_up, w_downs = [
        moved[i * local_count : (i + 1) * local_count] for i in range(3)
    ]
    hidden = []
    for k in range(local_count):
        gate_act = jnp.dot(rows_all, w_gate[k], preferred_element_type=jnp.float32)
        up_act = jnp.dot(rows_all, w_up[k], preferred_element_type=jnp.float32)
        hidden.append(
            (jax.nn.silu(gate_act) * up_act * own_shares[k]).astype(jnp.bfloat16)
        )
    sums = [None, None]
    for k in range(local_count):
        w_down = w_downs[k]
        for index, part_side in enumerate((1 - side, side)):
            w_part = lax.dynamic_slice_in_dim(w_down, part_side * half, half, axis=0)
            part = lax.dot_general(
                hidden[k], w_part, (((1,), (1,)), ((), ())), preferred_element_type=jnp.float32
            )
            sums[index] = part if sums[index] is None else sums[index] + part
    given, kept = sums
    kept = kept + swap(given.astype(jnp.bfloat16), "tensor", 1).astype(jnp.float32)
    out = jnp.concatenate(
        [
            halved(kept[:, :quarter], orders[0], block),
            halved(kept[:, quarter:], orders[1], block),
        ],
        axis=1,
    )
    return out.astype(jnp.bfloat16).reshape(step_count, row_count, half)


def solution(mesh):
    return jax.shard_map(
        local,
        mesh=mesh,
        in_specs=(
            P(None, ("groups", "expert"), None),
            P(None, ("groups", "expert"), None),
            P(None, ("groups", "expert"), None),
            P(None, ("groups", "expert", "tensor"), None),
            P(None, ("groups", "expert", "tensor"), None),
            P(None, ("groups", "expert", "tensor"), None),
        ),
        out_specs=P(None, ("groups", "expert"), "tensor"),
        check_vma=False,
    )
```

```python
import jax
import jax.numpy as jnp
from jax import lax
from jax.sharding import PartitionSpec as P

ALL = ("expert", "tensor")


def swap(value, axis, distance):
    count = lax.axis_size(axis)
    return lax.ppermute(value, axis, [(i, i ^ distance) for i in range(count)])


def orders_of(owners):
    bits = [bit for bit in range(owners.bit_length() - 1)][::-1]
    return bits, bits[:1] + bits[1:][::-1]


def doubled(value, bit):
    return jnp.concatenate([value, swap(value, "expert", 1 << bit)], axis=bit)


def halved(value, order, block):
    value = value.reshape((2,) * len(order) + (block, value.shape[-1]))
    for bit in order[::-1]:
        near = lax.slice_in_dim(value, 0, 1, axis=bit)
        far = lax.slice_in_dim(value, 1, 2, axis=bit).astype(jnp.bfloat16)
        value = near + swap(far, "expert", 1 << bit).astype(jnp.float32)
    return value.reshape(block, value.shape[-1])


def local(tokens, routes, mixing, gate_weight, up_weight, down_weight):
    owners = lax.axis_size("expert")
    pairs = lax.axis_size("tensor")
    expert_count = gate_weight.shape[0]
    step_count, row_count, model_width = tokens.shape
    devices = owners * pairs
    local_count = expert_count // devices
    block = step_count * row_count
    half = model_width // pairs
    quarter = half // 2
    side = lax.axis_index("tensor")
    me = lax.axis_index("expert") * pairs + side
    orders = orders_of(owners)
    named = routes[..., None] == jnp.arange(expert_count, dtype=jnp.int32)
    shares = jnp.sum(jnp.where(named, mixing[..., None], 0.0), axis=2).reshape(block, expert_count)
    x_half = lax.dynamic_slice_in_dim(tokens.reshape(block, model_width), side * half, half, axis=1)
    ones = (1,) * len(orders[0])
    state = (
        x_half[:, :quarter].reshape(ones + (block, quarter)),
        x_half[:, quarter:].reshape(ones + (block, half - quarter)),
        shares.reshape(ones + (block, expert_count)),
    )

    def advance(state, stage):
        if stage < len(orders[0]):
            first, second = orders[0][stage], orders[1][stage]
            return doubled(state[0], first), doubled(state[1], second), doubled(state[2], first)
        x_half = jnp.concatenate(
            [state[0].reshape(-1, quarter), state[1].reshape(-1, half - quarter)], axis=1
        )
        return x_half, swap(x_half, "tensor", 1), state[2].reshape(-1, expert_count)

    stages = len(orders[0]) + 1
    pieces = [gate_weight.reshape(devices, local_count, *gate_weight.shape[1:])]
    for weight in (up_weight, down_weight):
        parts = weight.reshape(devices, local_count, *weight.shape[1:])
        pieces += [parts[:, k] for k in range(local_count)]
    moved = []
    for index, piece in enumerate(pieces):
        if index > 0 and index <= stages:
            piece, state, moved[-1] = lax.optimization_barrier((piece, state, moved[-1]))
        elif index > 0:
            piece, moved[-1] = lax.optimization_barrier((piece, moved[-1]))
        if index < stages:
            state = advance(state, index)
        moved.append(lax.all_to_all(piece, ALL, split_axis=0, concat_axis=0, tiled=True))
    for stage in range(len(pieces), stages):
        state = advance(state, stage)
    x_half, x_other, shares = state
    rows_all = jnp.concatenate(
        [jnp.where(side == 0, x_half, x_other), jnp.where(side == 0, x_other, x_half)], axis=1
    )
    own_shares = lax.dynamic_slice_in_dim(shares, me * local_count, local_count, axis=1)
    moved = [moved[0][:, k] for k in range(local_count)] + moved[1:]
    moved = [value.reshape(model_width, value.shape[2]) for value in moved]
    w_gate, w_up, w_downs = [
        moved[i * local_count : (i + 1) * local_count] for i in range(3)
    ]
    hidden = []
    for k in range(local_count):
        gate_act = jnp.dot(rows_all, w_gate[k], preferred_element_type=jnp.float32)
        up_act = jnp.dot(rows_all, w_up[k], preferred_element_type=jnp.float32)
        hidden.append(
            (jax.nn.silu(gate_act) * up_act * own_shares[:, k : k + 1]).astype(jnp.bfloat16)
        )
    sums = [None, None]
    for k in range(local_count):
        w_down = w_downs[k]
        for index, part_side in enumerate((1 - side, side)):
            w_part = lax.dynamic_slice_in_dim(w_down, part_side * half, half, axis=0)
            part = lax.dot_general(
                hidden[k], w_part, (((1,), (1,)), ((), ())), preferred_element_type=jnp.float32
            )
            sums[index] = part if sums[index] is None else sums[index] + part
    given, kept = sums
    kept = kept + swap(given.astype(jnp.bfloat16), "tensor", 1).astype(jnp.float32)
    out = jnp.concatenate(
        [
            halved(kept[:, :quarter], orders[0], block),
            halved(kept[:, quarter:], orders[1], block),
        ],
        axis=1,
    )
    return out.astype(jnp.bfloat16).reshape(step_count, row_count, half)


def solution(mesh):
    return jax.shard_map(
        local,
        mesh=mesh,
        in_specs=(
            P(None, ("groups", "expert"), None),
            P(None, ("groups", "expert"), None),
            P(None, ("groups", "expert"), None),
            P(None, ("groups", "expert", "tensor"), None),
            P(None, ("groups", "expert", "tensor"), None),
            P(None, ("groups", "expert", "tensor"), None),
        ),
        out_specs=P(None, ("groups", "expert"), "tensor"),
        check_vma=False,
    )
```

```python
import jax
import jax.numpy as jnp
from jax import lax
from jax.sharding import PartitionSpec as P

ALL = ("expert", "tensor")


def swap(value, axis, distance):
    count = lax.axis_size(axis)
    return lax.ppermute(value, axis, [(i, i ^ distance) for i in range(count)])


def orders_of(owners):
    bits = [bit for bit in range(owners.bit_length() - 1)][::-1]
    return bits, bits[:1] + bits[1:][::-1]


def doubled(value, bit):
    return jnp.concatenate([value, swap(value, "expert", 1 << bit)], axis=bit)


def halved(value, order, block):
    value = value.reshape((2,) * len(order) + (block, value.shape[-1]))
    for bit in order[::-1]:
        near = lax.slice_in_dim(value, 0, 1, axis=bit)
        far = lax.slice_in_dim(value, 1, 2, axis=bit).astype(jnp.bfloat16)
        value = near + swap(far, "expert", 1 << bit).astype(jnp.float32)
    return value.reshape(block, value.shape[-1])


def local(tokens, routes, mixing, gate_weight, up_weight, down_weight):
    owners = lax.axis_size("expert")
    pairs = lax.axis_size("tensor")
    expert_count = gate_weight.shape[0]
    step_count, row_count, model_width = tokens.shape
    devices = owners * pairs
    local_count = expert_count // devices
    block = step_count * row_count
    half = model_width // pairs
    quarter = half // 2
    side = lax.axis_index("tensor")
    me = lax.axis_index("expert") * pairs + side
    orders = orders_of(owners)
    named = routes[..., None] == jnp.arange(expert_count, dtype=jnp.int32)
    shares = jnp.sum(jnp.where(named, mixing[..., None], 0.0), axis=2).reshape(block, expert_count)
    x_half = lax.dynamic_slice_in_dim(tokens.reshape(block, model_width), side * half, half, axis=1)
    ones = (1,) * len(orders[0])
    state = (
        x_half[:, :quarter].reshape(ones + (block, quarter)),
        x_half[:, quarter:].reshape(ones + (block, half - quarter)),
        shares.reshape(ones + (block, expert_count)),
    )

    def advance(state, stage):
        if stage < len(orders[0]):
            first, second = orders[0][stage], orders[1][stage]
            return doubled(state[0], first), doubled(state[1], second), doubled(state[2], first)
        x_half = jnp.concatenate(
            [state[0].reshape(-1, quarter), state[1].reshape(-1, half - quarter)], axis=1
        )
        return x_half, swap(x_half, "tensor", 1), state[2].reshape(-1, expert_count)

    stages = len(orders[0]) + 1
    gate_parts, up_parts, down_parts = [
        weight.reshape(devices, local_count, *weight.shape[1:])
        for weight in (gate_weight, up_weight, down_weight)
    ]
    pieces = [gate_parts, up_parts] + [down_parts[:, k] for k in range(local_count)]
    moved = []
    for index, piece in enumerate(pieces):
        if index > 0 and index <= stages:
            piece, state, moved[-1] = lax.optimization_barrier((piece, state, moved[-1]))
        elif index > 0:
            piece, moved[-1] = lax.optimization_barrier((piece, moved[-1]))
        if index < stages:
            state = advance(state, index)
        moved.append(lax.all_to_all(piece, ALL, split_axis=0, concat_axis=0, tiled=True))
    for stage in range(len(pieces), stages):
        state = advance(state, stage)
    x_half, x_other, shares = state
    rows_all = jnp.concatenate(
        [jnp.where(side == 0, x_half, x_other), jnp.where(side == 0, x_other, x_half)], axis=1
    )
    own_shares = lax.dynamic_slice_in_dim(shares, me * local_count, local_count, axis=1)
    moved = [both[:, k] for both in moved[:2] for k in range(local_count)] + moved[2:]
    moved = [value.reshape(model_width, value.shape[2]) for value in moved]
    w_gate, w_up, w_downs = [
        moved[i * local_count : (i + 1) * local_count] for i in range(3)
    ]
    hidden = []
    for k in range(local_count):
        gate_act = jnp.dot(rows_all, w_gate[k], preferred_element_type=jnp.float32)
        up_act = jnp.dot(rows_all, w_up[k], preferred_element_type=jnp.float32)
        hidden.append(
            (jax.nn.silu(gate_act) * up_act * own_shares[:, k : k + 1]).astype(jnp.bfloat16)
        )
    sums = [None, None]
    for k in range(local_count):
        w_down = w_downs[k]
        for index, part_side in enumerate((1 - side, side)):
            w_part = lax.dynamic_slice_in_dim(w_down, part_side * half, half, axis=0)
            part = lax.dot_general(
                hidden[k], w_part, (((1,), (1,)), ((), ())), preferred_element_type=jnp.float32
            )
            sums[index] = part if sums[index] is None else sums[index] + part
    given, kept = sums
    kept = kept + swap(given.astype(jnp.bfloat16), "tensor", 1).astype(jnp.float32)
    out = jnp.concatenate(
        [
            halved(kept[:, :quarter], orders[0], block),
            halved(kept[:, quarter:], orders[1], block),
        ],
        axis=1,
    )
    return out.astype(jnp.bfloat16).reshape(step_count, row_count, half)


def solution(mesh):
    return jax.shard_map(
        local,
        mesh=mesh,
        in_specs=(
            P(None, ("groups", "expert"), None),
            P(None, ("groups", "expert"), None),
            P(None, ("groups", "expert"), None),
            P(None, ("groups", "expert", "tensor"), None),
            P(None, ("groups", "expert", "tensor"), None),
            P(None, ("groups", "expert", "tensor"), None),
        ),
        out_specs=P(None, ("groups", "expert"), "tensor"),
        check_vma=False,
    )
```
